32 devices in a mesh: gx: 8 (over z, y), gy: 4 (over x, core).
Axes of the slice: x: 2, y: 2, z: 4, core: 2. Of those that a mesh axis runs over, the one named last changes fastest.
Arguments:
- latent: bfloat16 [32, 512, 128], P('gx', 'gy'), may hold values from -6 to 6
- corr_kernel: bfloat16 [32, 128], replicated, may hold values from -1 to 1
- first_conv_weight: bfloat16 [3, 3, 128, 128], replicated, may hold values from -0.1875 to 0.1875
- first_conv_bias: float32 [128], replicated, may hold values from -3 to 3
- second_conv_weight: bfloat16 [3, 3, 128, 128], replicated, may hold values from -0.1875 to 0.1875
- second_conv_bias: float32 [128], replicated, may hold values from -3 to 3
- cotangent: bfloat16 [32, 512, 128], P('gx', 'gy'), may hold values from -0.046875 to 0.046875
Outputs:
- prediction: bfloat16 [32, 512, 128], P('gx', 'gy')
- conv1_weight_grad: float32 [3, 3, 128, 128], replicated
- conv1_bias_grad: float32 [128], replicated
- conv2_weight_grad: float32 [3, 3, 128, 128], replicated
- conv2_bias_grad: float32 [128], replicated
- kernel_grad: float32 [32, 128], replicated
The draws below stay inside these ranges and needn't reach their ends.
All inputs are finite; a program needn't handle non-finite values.
Results may differ from the reference program's by a relative error of at most 0.0095.
Values may be sent and summed in bfloat16 or wider, within the bound.
A program may use at most 64 MiB of HBM per device.

```python
import jax
import jax.numpy as jnp
from jax import lax

C = 128
DILATION_FIRST = 1
DILATION_SECOND = 2
NX = 32
NY = 512


def steps_of(own_key, dims, split, low, high):
    def one(axis_at, shards_of):
        heights = jax.random.uniform(jax.random.fold_in(jax.random.fold_in(own_key, 6), axis_at), (shards_of,), jnp.float32, low / len(split), high / len(split))
        return jnp.repeat(jnp.exp(heights), dims[axis_at] // shards_of).reshape((-1,) + (1,) * (len(dims) - axis_at - 1))

    factor_of = one(*split[0])
    for cut in split[1:]:
        factor_of = factor_of * one(*cut)
    return factor_of


def bell_draw(rng, shape, deviation, limit, cuts=(), kind=jnp.bfloat16):
    factor_of = steps_of(rng, shape, cuts, -0.22, 0.18) if cuts else 1.0
    entries = jax.random.normal(rng, shape, jnp.float32) * deviation * factor_of
    return jnp.minimum(jnp.maximum(entries, -limit), limit).astype(kind)


def setup_inputs(seed: int = 0) -> dict:
    splits = jax.random.split(jax.random.key(seed), 8)
    latent = bell_draw(splits[0], (NX, NY, C), 1.0, 6.0, ((0, 8), (1, 4)))
    corr_kernel = bell_draw(splits[1], (NX, C), NX ** -0.5, 1.0)
    first_conv_weight = bell_draw(splits[2], (3, 3, C, C), (9 * C) ** -0.5, 0.1875)
    first_conv_bias = bell_draw(splits[3], (C,), 0.5, 3.0, (), jnp.float32)
    second_conv_weight = bell_draw(splits[4], (3, 3, C, C), (9 * C) ** -0.5, 0.1875)
    second_conv_bias = bell_draw(splits[5], (C,), 0.5, 3.0, (), jnp.float32)
    cotangent = bell_draw(splits[6], (NX, NY, C), (1.0 / (NX * NY) ** 0.5), 0.046875, ((0, 8), (1, 4)))
    return dict(latent=latent, corr_kernel=corr_kernel, first_conv_weight=first_conv_weight, first_conv_bias=first_conv_bias, second_conv_weight=second_conv_weight, second_conv_bias=second_conv_bias, cotangent=cotangent)


def silu_slope(preact):
    logistic = jax.nn.sigmoid(preact)
    return logistic * (1.0 + preact * (1.0 - logistic))


def correlate_rows(latent, corr_kernel):
    blocks_out = []
    for block_start in range(0, C, 16):
        field = latent[:, :, block_start:block_start + 16].astype(jnp.float32)
        kernel_part = corr_kernel[:, block_start:block_start + 16].astype(jnp.float32)
        spectrum = jnp.fft.fft(field, axis=0) * jnp.conj(jnp.fft.fft(kernel_part, axis=0))[:, None, :]
        blocks_out.append(jnp.real(jnp.fft.ifft(spectrum, axis=0)))
    return jnp.concatenate(blocks_out, axis=-1)


def kernel_gradient(mixed_gradient, latent):
    blocks_out = []
    for block_start in range(0, C, 16):
        grad_part = jnp.fft.fft(mixed_gradient[:, :, block_start:block_start + 16].astype(jnp.float32), axis=0)
        field_part = jnp.fft.fft(latent[:, :, block_start:block_start + 16].astype(jnp.float32), axis=0)
        cross = jnp.sum(jnp.conj(grad_part) * field_part, axis=1)
        blocks_out.append(jnp.real(jnp.fft.ifft(cross, axis=0)))
    return jnp.concatenate(blocks_out, axis=-1)


def dilated_conv_apply(field, weight, bias_vec, dilation):
    running = jnp.zeros((NX * NY, C), jnp.float32) + bias_vec
    for row_off in (-1, 0, 1):
        for col_off in (-1, 0, 1):
            moved = jnp.roll(field, (-row_off * dilation, -col_off * dilation), axis=(0, 1))
            running = running + jnp.dot(moved.reshape(-1, C), weight[row_off + 1, col_off + 1], preferred_element_type=jnp.float32)
    return running.reshape(NX, NY, C)


def dilated_conv_weight_gradient(field, slope, dilation):
    flat_slope = slope.reshape(-1, C)
    rows_out = []
    for row_off in (-1, 0, 1):
        cols_out = []
        for col_off in (-1, 0, 1):
            moved = jnp.roll(field, (-row_off * dilation, -col_off * dilation), axis=(0, 1)).reshape(-1, C)
            cols_out.append(lax.dot_general(moved, flat_slope, (((0,), (0,)), ((), ())), preferred_element_type=jnp.float32))
        rows_out.append(jnp.stack(cols_out))
    return jnp.stack(rows_out)


def dilated_conv_adjoint(slope, weight, dilation):
    running = jnp.zeros((NX * NY, C), jnp.float32)
    for row_off in (-1, 0, 1):
        for col_off in (-1, 0, 1):
            moved = jnp.roll(slope, (row_off * dilation, col_off * dilation), axis=(0, 1))
            running = running + jnp.dot(moved.reshape(-1, C), weight[row_off + 1, col_off + 1].T, preferred_element_type=jnp.float32)
    return running.reshape(NX, NY, C)


def reference(latent, corr_kernel, first_conv_weight, first_conv_bias, second_conv_weight, second_conv_bias, cotangent):
    mixed_field = (latent.astype(jnp.float32) + correlate_rows(latent, corr_kernel)).astype(jnp.bfloat16)
    first_preactivation = dilated_conv_apply(mixed_field, first_conv_weight, first_conv_bias, DILATION_FIRST)
    hidden_activation = (mixed_field.astype(jnp.float32) + jax.nn.silu(first_preactivation)).astype(jnp.bfloat16)
    second_preactivation = dilated_conv_apply(hidden_activation, second_conv_weight, second_conv_bias, DILATION_SECOND)
    prediction = (hidden_activation.astype(jnp.float32) + jax.nn.silu(second_preactivation)).astype(jnp.bfloat16)
    incoming_gradient = cotangent.astype(jnp.float32)
    second_activation_slope = (incoming_gradient * silu_slope(second_preactivation)).astype(jnp.bfloat16)
    second_weight_matrix = dilated_conv_weight_gradient(hidden_activation, second_activation_slope, DILATION_SECOND)
    bias_two = jnp.sum(second_activation_slope.astype(jnp.float32), axis=(0, 1))
    hidden_gradient = incoming_gradient + dilated_conv_adjoint(second_activation_slope, second_conv_weight, DILATION_SECOND)
    first_activation_slope = (hidden_gradient * silu_slope(first_preactivation)).astype(jnp.bfloat16)
    first_weight_matrix = dilated_conv_weight_gradient(mixed_field, first_activation_slope, DILATION_FIRST)
    bias_one = jnp.sum(first_activation_slope.astype(jnp.float32), axis=(0, 1))
    mixed_gradient = (hidden_gradient + dilated_conv_adjoint(first_activation_slope, first_conv_weight, DILATION_FIRST)).astype(jnp.bfloat16)
    kernel_grad = kernel_gradient(mixed_gradient, latent)
    return (prediction, first_weight_matrix, bias_one, second_weight_matrix, bias_two, kernel_grad)
```

```python
import functools

import jax
import jax.numpy as jnp
from jax import lax
from jax.experimental import pallas as pl
from jax.experimental.pallas import tpu as pltpu
from jax.sharding import PartitionSpec as P

D1 = 1
D2 = 2
EDGE = 16
BF = jnp.bfloat16
F32 = jnp.float32
MESH = pl.DeviceIdType.MESH


def sigmoid(v):
    return 1.0 / (1.0 + jnp.exp(-v))


def slope_of(v):
    g = sigmoid(v)
    return g * (1.0 + v * (1.0 - g))


def kernel(
    GX, GY, L, WC, C, CH1, CH2,
    lat_in, k_in, w1, b1, w2, b2, cot_in,
    pred, o2, o1, okern, ob1, ob2,
    lat, cot, kd, mix, xf, xs, xh, xg, pre1, hid, wt1, wt2,
    acc1, acc2, hacc1, hacc2, qacc1, qacc2,
    sa1, sa2, ra1, ra2, sb1, sb2, rb1, rb2, sc1, sc2, rc1, rc2, og1, og2,
    ring_s, ring_r, edge_s, edge_r, cot_s, cot_r,
    p1_s, p1_r, p2_s, p2_r, p3_s, p3_r, g3_s, g3_r, g2_s, g2_r, g1_s, g1_r,
):
    NX = L * GX
    W = WC + 2 * EDGE
    GA = GY // 2
    half_n = GX // 2
    gx = lax.axis_index("gx")
    gy = lax.axis_index("gy")
    core = lax.rem(gy, 2)
    ga = gy // 2

    odd = lax.rem(gx, 2)
    pos = (1 - odd) * (gx // 2) + odd * (GX - 1 - gx // 2)

    def at_pos(p):
        p = lax.rem(p + 2 * GX, GX)
        back = (p >= half_n).astype(jnp.int32)
        return (1 - back) * (2 * p) + back * (2 * (GX - 1 - p) + 1)

    right, left = at_pos(pos + 1), at_pos(pos - 1)
    up, down = lax.rem(gx + GX - 1, GX), lax.rem(gx + 1, GX)
    west, east = lax.rem(gy + GY - 1, GY), lax.rem(gy + 1, GY)
    mate = gy + 1 - 2 * core

    barrier = pltpu.get_barrier_semaphore()
    met = 0
    for d in range(1, GX):
        pl.semaphore_signal(barrier, inc=1, device_id=(lax.rem(gx + d, GX), gy), device_id_type=MESH)
        met += 1
    for d in range(1, GY):
        pl.semaphore_signal(barrier, inc=1, device_id=(gx, lax.rem(gy + d, GY)), device_id_type=MESH)
        met += 1
    for vertical in (up, down):
        for side in (west, east):
            pl.semaphore_signal(barrier, inc=1, device_id=(vertical, side), device_id_type=MESH)
            met += 1
    lat[pl.ds(L * gx, L), EDGE : EDGE + WC, :] = lat_in[...]
    pl.semaphore_wait(barrier, met)

    def copy(src, dst, send, recv, target):
        return pltpu.make_async_remote_copy(
            src_ref=src, dst_ref=dst, send_sem=send, recv_sem=recv,
            device_id=target, device_id_type=MESH,
        )

    hl = L // 2

    def ring(way, step, h):
        block = at_pos(pos - (step - 1)) if way == 0 else at_pos(pos + (step - 1))
        piece = lat.at[pl.ds(L * block + h * hl, hl), EDGE : EDGE + WC, :]
        target = (right, gy) if way == 0 else (left, gy)
        where = (way, step - 1, h)
        return copy(piece, piece, ring_s.at[where], ring_r.at[where], target)

    def goes(way, step, h):
        return step < half_n or (step == half_n and h == way)

    def edge(way, block):
        rows = pl.ds(L * block, L)
        if way == 0:
            src, dst, target = lat.at[rows, WC : WC + EDGE, :], lat.at[rows, 0:EDGE, :], (gx, east)
        else:
            src = lat.at[rows, EDGE : 2 * EDGE, :]
            dst, target = lat.at[rows, EDGE + WC : W, :], (gx, west)
        return copy(src, dst, edge_s.at[way, block], edge_r.at[way, block], target)

    for h in range(2):
        for way in range(2):
            ring(way, 1, h).start()
    for way in range(2):
        edge(way, gx).start()

    kd[0:NX, :] = k_in[...].astype(F32)
    kd[NX : 2 * NX, :] = k_in[...].astype(F32)
    cot[3 : 3 + L, EDGE : EDGE + WC, :] = cot_in[...]
    xf[0:8, :] = jnp.zeros((8, C), F32)
    xf[xf.shape[0] - 8 :, :] = jnp.zeros((8, C), F32)
    for p in range(3):
        for q in range(3):
            part = slice(q * C, (q + 1) * C)
            wt1[p, part, :] = w1[p, part, :].astype(F32).T.astype(BF)
            wt2[p, part, :] = w2[p, part, :].astype(F32).T.astype(BF)
    acc1[...] = jnp.zeros(acc1.shape, F32)
    acc2[...] = jnp.zeros(acc2.shape, F32)
    RM = L + 12
    mix[...] = jnp.zeros(mix.shape, F32)
    top = lax.rem(L * gx - 6 + 2 * NX, NX)

    def correlate(rows_at, count, tiles):
        base = lax.rem(rows_at - top + 2 * NX, NX)

        def tile(t, carry):
            col = pl.multiple_of(tiles[0] + t * tiles[1], 16)
            parts = [mix[m, pl.ds(col, 16), :] for m in range(RM)]
            for r in range(count):
                row = lax.rem(base + r, NX)
                value = lat[rows_at + r, pl.ds(col, 16), :].astype(F32)
                for m in range(RM):
                    factor = kd[pl.ds(lax.rem(row + (2 * NX - m), NX), 1), :]
                    parts[m] = parts[m] + value * factor
            for m in range(RM):
                mix[m, pl.ds(col, 16), :] = parts[m]
            return carry

        lax.fori_loop(0, tiles[2], tile, 0)

    center = (EDGE, 16, WC // 16)
    sides = (0, EDGE + WC, 2)
    correlate(L * gx, L, center)

    def cot_copy(i):
        rows_src = (slice(L - 3, L), slice(0, L), slice(0, 3))
        rows_dst = (slice(0, 3), slice(3, 3 + L), slice(3 + L, 6 + L))
        cols_src = (slice(WC - EDGE, WC), slice(0, WC), slice(0, EDGE))
        cols_dst = (slice(0, EDGE), slice(EDGE, EDGE + WC), slice(EDGE + WC, W))
        a, b = i // 3, i % 3
        target = ((down, gx, up)[a], (east, gy, west)[b])
        return copy(
            cot_in.at[rows_src[a], cols_src[b], :], cot.at[rows_dst[a], cols_dst[b], :],
            cot_s.at[i], cot_r.at[i], target,
        )

    cots = [i for i in range(9) if i != 4]
    for step in range(1, half_n + 1):
        for h in range(2):
            for way in range(2):
                if goes(way, step, h):
                    ring(way, step, h).wait_recv()
                    if goes(way, step + 1, h):
                        ring(way, step + 1, h).start()
        if step < half_n:
            blocks = [at_pos(pos - step), at_pos(pos + step)]
        else:
            blocks = [at_pos(pos + step)]
        for block in blocks:
            for way in range(2):
                edge(way, block).start()
        if step == half_n:
            for i in cots:
                cot_copy(i).start()
        for block in blocks:
            correlate(L * block, L, center)

    def late(block, carry):
        for way in range(2):
            edge(way, block).wait_recv()
        return carry

    lax.fori_loop(0, GX, late, 0)

    def late_rows(block, carry):
        correlate(L * block, L, sides)
        return carry

    lax.fori_loop(0, GX, late_rows, 0)

    def flat(ref):
        return ref[...].reshape(-1, C)

    def widen(target, value, rows, dil):
        m = rows * W
        xf[8 : 8 + m, :] = value
        for q in range(3):
            at = 8 + (q - 1) * dil
            target[0:m, q * C : (q + 1) * C] = xf[at : at + m, :].astype(BF)

    def rows_dot(source, starts, weight, rows):
        total = None
        for p in range(3):
            at = starts[p] * W
            term = jnp.dot(source[at : at + rows * W, :], weight[p], preferred_element_type=F32)
            total = term if total is None else total + term
        return total

    def weight_grad(source, starts, slope_own, p):
        at = starts[p]
        taps = jnp.concatenate(
            [source[(at + i) * W + EDGE : (at + i) * W + EDGE + WC, :] for i in range(L)], axis=0
        )
        return lax.dot_general(taps, slope_own, (((0,), (0,)), ((), ())), preferred_element_type=F32)

    def own(value, start):
        return jnp.concatenate(
            [value[(start + i) * W + EDGE : (start + i) * W + EDGE + WC, :] for i in range(L)], axis=0
        )

    for m in range(RM):
        row = lat[lax.rem(top + m, NX), :, :].astype(F32)
        mix[m] = (row + mix[m]).astype(BF).astype(F32)

    R1 = L + 10
    widen(xs, flat(mix), RM, D1)
    pre1[...] = rows_dot(xs, (0, 1, 2), w1, R1) + b1[...]
    v = pre1[...]
    mixed_in = mix[1 : 1 + R1].reshape(-1, C)
    hid[...] = (mixed_in + v * sigmoid(v)).astype(BF).astype(F32)
    R2 = L + 6
    widen(xh, hid[...], R1, D2)
    pre2 = rows_dot(xh, (0, 2, 4), w2, R2) + b2[...]
    own2 = own(pre2, 3)
    own_hid = own(hid, 5)
    pred[...] = (own_hid + own2 * sigmoid(own2)).astype(BF).reshape(L, WC, C)
    for i in cots:
        cot_copy(i).wait_recv()
    slope2 = (flat(cot).astype(F32) * slope_of(pre2)).astype(BF).astype(F32)
    own_slope2 = own(slope2, 3)
    grad2 = [weight_grad(xh, (3, 5, 7), own_slope2.astype(BF), p) for p in range(3)]
    SIZE = 9 * C
    first = min(acc1.shape[0], SIZE)

    def put_second(p):
        lo, hi = p * 3 * C, (p + 1) * 3 * C
        cut = min(max(first, lo), hi)
        if cut > lo:
            acc1[lo:cut, :] = grad2[p][: cut - lo]
        if cut < hi:
            acc2[cut - first : hi - first, :] = grad2[p][cut - lo :]

    for p in range(3):
        put_second(p)

    class Stream:
        pass

    streams = []
    for k in range(2):
        s = Stream()
        s.k = k
        s.ch = (CH1, CH2)[k]
        s.acc, s.hacc, s.qacc = (acc1, acc2)[k], (hacc1, hacc2)[k], (qacc1, qacc2)[k]
        s.sa, s.ra = (sa1, sa2)[k], (ra1, ra2)[k]
        s.sb, s.rb = (sb1, sb2)[k], (rb1, rb2)[k]
        s.sc, s.rc, s.og = (sc1, sc2)[k], (rc1, rc2)[k], (og1, og2)[k]
        s.quarter = GX * s.ch
        s.half = GA * s.quarter
        streams.append(s)

    def ds(at, size):
        return pl.ds(pl.multiple_of(at, 16), size)

    def p1(s):
        return copy(s.sa, s.ra, p1_s.at[s.k], p1_r.at[s.k], (gx, mate))

    def p2(s, d):
        other = lax.rem(ga + d, GA)
        return copy(s.sb.at[ds(other * s.quarter, s.quarter), :], s.rb.at[d],
                    p2_s.at[s.k, d], p2_r.at[s.k, d], (gx, 2 * other + core))

    def p3(s, d):
        other = lax.rem(gx + d, GX)
        return copy(s.sc.at[ds(other * s.ch, s.ch), :], s.rc.at[d],
                    p3_s.at[s.k, d], p3_r.at[s.k, d], (other, gy))

    def g3(s, d, send):
        owner = gx if send else lax.rem(gx + GX - d, GX)
        piece = s.og.at[ds(core * s.half + ga * s.quarter + owner * s.ch, s.ch), :]
        return copy(piece, piece, g3_s.at[s.k, d], g3_r.at[s.k, d], (lax.rem(gx + d, GX), gy))

    def g2(s, d, send):
        owner = ga if send else lax.rem(ga + GA - d, GA)
        piece = s.og.at[ds(core * s.half + owner * s.quarter, s.quarter), :]
        return copy(piece, piece, g2_s.at[s.k, d], g2_r.at[s.k, d],
                    (gx, 2 * lax.rem(ga + d, GA) + core))

    def g1(s, send):
        owner = core if send else 1 - core
        piece = s.og.at[ds(owner * s.half, s.half), :]
        return copy(piece, piece, g1_s.at[s.k], g1_r.at[s.k], (gx, mate))

    def begin(s):
        s.sa[...] = s.acc[ds((1 - core) * s.half, s.half), :].astype(BF)
        p1(s).start()

    def after_one(s):
        p1(s).wait_recv()
        total = s.acc[ds(core * s.half, s.half), :] + s.ra[...].astype(F32)
        s.hacc[...] = total
        s.sb[...] = total.astype(BF)
        for d in range(1, GA):
            p2(s, d).start()

    def after_two(s):
        total = s.hacc[ds(ga * s.quarter, s.quarter), :]
        for d in range(1, GA):
            p2(s, d).wait_recv()
            total = total + s.rb[d].astype(F32)
        s.qacc[...] = total
        s.sc[...] = total.astype(BF)
        for d in range(1, GX):
            p3(s, d).start()

    def after_three(s):
        total = s.qacc[ds(gx * s.ch, s.ch), :]
        for d in range(1, GX):
            p3(s, d).wait_recv()
            total = total + s.rc[d].astype(F32)
        s.og[ds(core * s.half + ga * s.quarter + gx * s.ch, s.ch), :] = total.astype(BF)
        for d in range(1, GX):
            g3(s, d, True).start()

    def gather_two(s):
        for d in range(1, GX):
            g3(s, d, False).wait_recv()
        for d in range(1, GA):
            g2(s, d, True).start()

    def gather_one(s):
        for d in range(1, GA):
            g2(s, d, False).wait_recv()
        g1(s, True).start()

    one, two = streams
    begin(one)

    R3 = L + 2
    widen(xg, slope2, R2, -D2)
    back2 = rows_dot(xg, (4, 2, 0), wt2, R3)
    grad_hid = flat(cot)[2 * W : (2 + R3) * W].astype(F32) + back2
    slope1 = (grad_hid * slope_of(pre1[4 * W : (4 + R3) * W, :])).astype(BF).astype(F32)
    after_one(one)
    own_slope1 = own(slope1, 1)
    shift = SIZE - first
    for p in range(3):
        lo = shift + p * 3 * C
        acc2[lo : lo + 3 * C, :] = weight_grad(xs, (5, 6, 7), own_slope1.astype(BF), p)
    widen(xg, slope1, R3, -D1)
    grad_mixed = grad_hid[W : (1 + L) * W] + rows_dot(xg, (2, 1, 0), wt1, L)
    mix[0:L, EDGE : EDGE + WC, :] = own(grad_mixed, 0).astype(BF).astype(F32).reshape(L, WC, C)
    misc = shift + SIZE

    def kernel_row(o, carry):
        total = jnp.zeros((16, C), F32)
        for i in range(L):
            row = lax.rem(L * gx + i + o, NX)
            for t in range(WC // 16):
                cols = slice(EDGE + t * 16, EDGE + (t + 1) * 16)
                total = total + mix[i, cols, :] * lat[row, cols, :].astype(F32)
        acc2[pl.ds(misc + o, 1), :] = jnp.sum(total, axis=0, keepdims=True)
        return carry

    lax.fori_loop(0, NX, kernel_row, 0)
    acc2[misc + NX : misc + NX + 1, :] = jnp.sum(own_slope1, axis=0, keepdims=True)
    acc2[misc + NX + 8 : misc + NX + 9, :] = jnp.sum(own_slope2, axis=0, keepdims=True)

    begin(two)
    after_two(one)
    after_one(two)
    after_three(one)
    after_two(two)
    gather_two(one)
    after_three(two)
    gather_one(one)
    gather_two(two)
    gather_one(two)
    g1(one, False).wait_recv()
    o2[0:first, :] = og1[0:first, :]
    g1(two, False).wait_recv()
    if first < SIZE:
        o2[first:SIZE, :] = og2[0:shift, :]
    o1[...] = og2[shift : shift + SIZE, :]
    okern[...] = og2[misc : misc + NX, :].astype(F32)
    tail = og2[misc + NX : misc + NX + 16, :].astype(F32)
    ob1[...] = tail[0:1]
    ob2[...] = tail[8:9]

    for step in range(1, half_n + 1):
        for h in range(2):
            for way in range(2):
                if goes(way, step, h):
                    ring(way, step, h).wait_send()

    def sent(block, carry):
        for way in range(2):
            edge(way, block).wait_send()
        return carry

    lax.fori_loop(0, GX, sent, 0)
    for i in cots:
        cot_copy(i).wait_send()
    for s in streams:
        p1(s).wait_send()
        for d in range(1, GA):
            p2(s, d).wait_send()
            g2(s, d, True).wait_send()
        for d in range(1, GX):
            p3(s, d).wait_send()
            g3(s, d, True).wait_send()
        g1(s, True).wait_send()


def per_device(latent, corr_kernel, w1, b1, w2, b2, cotangent):
    GX, GY = lax.axis_size("gx"), lax.axis_size("gy")
    L, WC, C = latent.shape
    NX = L * GX
    W = WC + 2 * EDGE
    N = GX * GY
    GA = GY // 2
    SIZE = 9 * C
    CH1 = max(16, SIZE // (16 * N) * 16)
    rest = SIZE - min(SIZE, CH1 * N) + SIZE + NX + 16
    CH2 = -(-rest // (16 * N)) * 16
    dma = pltpu.SemaphoreType.DMA

    def pair(shape_of, kind):
        return [pltpu.VMEM(shape_of(ch), kind) for ch in (CH1, CH2)]

    scratch = [
        pltpu.VMEM((NX, W, C), BF),
        pltpu.VMEM((L + 6, W, C), BF),
        pltpu.VMEM((2 * NX, C), F32),
        pltpu.VMEM((L + 12, W, C), F32),
        pltpu.VMEM(((L + 12) * W + 16, C), F32),
        pltpu.VMEM(((L + 12) * W, 3 * C), BF),
        pltpu.VMEM(((L + 10) * W, 3 * C), BF),
        pltpu.VMEM(((L + 6) * W, 3 * C), BF),
        pltpu.VMEM(((L + 10) * W, C), F32),
        pltpu.VMEM(((L + 10) * W, C), F32),
        pltpu.VMEM((3, 3 * C, C), BF),
        pltpu.VMEM((3, 3 * C, C), BF),
        *pair(lambda ch: (N * ch, C), F32),
        *pair(lambda ch: (GA * GX * ch, C), F32),
        *pair(lambda ch: (GX * ch, C), F32),
        *pair(lambda ch: (GA * GX * ch, C), BF),
        *pair(lambda ch: (GA * GX * ch, C), BF),
        *pair(lambda ch: (GA * GX * ch, C), BF),
        *pair(lambda ch: (GA, GX * ch, C), BF),
        *pair(lambda ch: (GX * ch, C), BF),
        *pair(lambda ch: (GX, ch, C), BF),
        *pair(lambda ch: (N * ch, C), BF),
        dma((2, GX // 2, 2)), dma((2, GX // 2, 2)),
        dma((2, GX)), dma((2, GX)),
        dma((9,)), dma((9,)),
        dma((2,)), dma((2,)),
        dma((2, GA)), dma((2, GA)),
        dma((2, GX)), dma((2, GX)),
        dma((2, GX)), dma((2, GX)),
        dma((2, GA)), dma((2, GA)),
        dma((2,)), dma((2,)),
    ]
    vmem = pl.BlockSpec(memory_space=pltpu.VMEM)
    pred, g2, g1, gk, gb1, gb2 = pl.pallas_call(
        functools.partial(kernel, GX, GY, L, WC, C, CH1, CH2),
        out_shape=(
            jax.ShapeDtypeStruct((L, WC, C), BF),
            jax.ShapeDtypeStruct((SIZE, C), BF),
            jax.ShapeDtypeStruct((SIZE, C), BF),
            jax.ShapeDtypeStruct((NX, C), F32),
            jax.ShapeDtypeStruct((1, C), F32),
            jax.ShapeDtypeStruct((1, C), F32),
        ),
        in_specs=[vmem] * 7,
        out_specs=[vmem] * 6,
        scratch_shapes=scratch,
        compiler_params=pltpu.CompilerParams(
            collective_id=0, has_side_effects=True, vmem_limit_bytes=56 * 1024 * 1024
        ),
        cost_estimate=pl.CostEstimate(
            flops=2 * 6 * 10 * W * SIZE * C, bytes_accessed=4 * SIZE * C * 2, transcendentals=24 * W * C
        ),
    )(
        latent, corr_kernel, w1.reshape(3, 3 * C, C), b1.reshape(1, C),
        w2.reshape(3, 3 * C, C), b2.reshape(1, C), cotangent,
    )
    shape = (3, 3, C, C)
    return (
        pred,
        g1.astype(F32).reshape(shape), gb1.reshape(C),
        g2.astype(F32).reshape(shape), gb2.reshape(C),
        gk,
    )


def solution(mesh):
    in_specs = (P("gx", "gy", None), P(), P(), P(), P(), P(), P("gx", "gy", None))
    out_specs = (P("gx", "gy", None), P(), P(), P(), P(), P())
    return jax.shard_map(
        per_device, mesh=mesh, in_specs=in_specs, out_specs=out_specs, check_vma=False
    )
```

```python
import functools

import jax
import jax.numpy as jnp
from jax import lax
from jax.experimental import pallas as pl
from jax.experimental.pallas import tpu as pltpu
from jax.sharding import PartitionSpec as P

D1 = 1
D2 = 2
EDGE = 16
BF = jnp.bfloat16
F32 = jnp.float32
MESH = pl.DeviceIdType.MESH


def sigmoid(v):
    return 1.0 / (1.0 + jnp.exp(-v))


def slope_of(v):
    g = sigmoid(v)
    return g * (1.0 + v * (1.0 - g))


def kernel(
    GX, GY, L, WC, C, CH1, CH2,
    lat_in, k_in, w1, b1, w2, b2, cot_in,
    pred, o2, o1, orest,
    lat, cot, kd, mix, xf, xs, xh, xg, pre1, hid, wt1, wt2,
    acc1, acc2, hacc1, hacc2, qacc1, qacc2,
    sa1, sa2, ra1, ra2, sb1, sb2, rb1, rb2, sc1, sc2, rc1, rc2, og1, og2,
    ring_s, ring_r, edge_s, edge_r, cot_s, cot_r,
    p1_s, p1_r, p2_s, p2_r, p3_s, p3_r, g3_s, g3_r, g2_s, g2_r, g1_s, g1_r,
):
    NX = L * GX
    W = WC + 2 * EDGE
    GA = GY // 2
    half_n = GX // 2
    gx = lax.axis_index("gx")
    gy = lax.axis_index("gy")
    core = lax.rem(gy, 2)
    ga = gy // 2

    odd = lax.rem(gx, 2)
    pos = (1 - odd) * (gx // 2) + odd * (GX - 1 - gx // 2)

    def at_pos(p):
        p = lax.rem(p + 2 * GX, GX)
        back = (p >= half_n).astype(jnp.int32)
        return (1 - back) * (2 * p) + back * (2 * (GX - 1 - p) + 1)

    right, left = at_pos(pos + 1), at_pos(pos - 1)
    up, down = lax.rem(gx + GX - 1, GX), lax.rem(gx + 1, GX)
    west, east = lax.rem(gy + GY - 1, GY), lax.rem(gy + 1, GY)
    mate = gy + 1 - 2 * core

    barrier = pltpu.get_barrier_semaphore()
    met = 0
    for d in range(1, GX):
        pl.semaphore_signal(barrier, inc=1, device_id=(lax.rem(gx + d, GX), gy), device_id_type=MESH)
        met += 1
    for d in range(1, GY):
        pl.semaphore_signal(barrier, inc=1, device_id=(gx, lax.rem(gy + d, GY)), device_id_type=MESH)
        met += 1
    for vertical in (up, down):
        for side in (west, east):
            pl.semaphore_signal(barrier, inc=1, device_id=(vertical, side), device_id_type=MESH)
            met += 1
    lat[pl.ds(L * gx, L), EDGE : EDGE + WC, :] = lat_in[...]
    pl.semaphore_wait(barrier, met)

    def copy(src, dst, send, recv, target):
        return pltpu.make_async_remote_copy(
            src_ref=src, dst_ref=dst, send_sem=send, recv_sem=recv,
            device_id=target, device_id_type=MESH,
        )

    hl = L // 2

    def ring(way, step, h):
        block = at_pos(pos - (step - 1)) if way == 0 else at_pos(pos + (step - 1))
        piece = lat.at[pl.ds(L * block + h * hl, hl), EDGE : EDGE + WC, :]
        target = (right, gy) if way == 0 else (left, gy)
        where = (way, step - 1, h)
        return copy(piece, piece, ring_s.at[where], ring_r.at[where], target)

    def goes(way, step, h):
        return step < half_n or (step == half_n and h == way)

    def edge(way, block):
        rows = pl.ds(L * block, L)
        if way == 0:
            src, dst, target = lat.at[rows, WC : WC + EDGE, :], lat.at[rows, 0:EDGE, :], (gx, east)
        else:
            src = lat.at[rows, EDGE : 2 * EDGE, :]
            dst, target = lat.at[rows, EDGE + WC : W, :], (gx, west)
        return copy(src, dst, edge_s.at[way, block], edge_r.at[way, block], target)

    for h in range(2):
        for way in range(2):
            ring(way, 1, h).start()
    for way in range(2):
        edge(way, gx).start()

    spread = jnp.broadcast_to(k_in[...].astype(F32)[:, None, :], (NX, 8, C))
    for i in range(3):
        kd[i * NX : (i + 1) * NX, :, :] = spread
    cot[3 : 3 + L, EDGE : EDGE + WC, :] = cot_in[...]
    xf[0:8, :] = jnp.zeros((8, C), F32)
    xf[xf.shape[0] - 8 :, :] = jnp.zeros((8, C), F32)

    def turn(target, weight):
        for p in range(3):
            for q in range(3):
                from_at, to_at = (3 * p + q) * C, (3 * (2 - p) + q) * C
                target[to_at : to_at + C, :] = weight[from_at : from_at + C, :].astype(F32).T.astype(BF)

    def prepare(step):
        if step == 1:
            turn(wt2, w2)
        if step == min(2, half_n):
            turn(wt1, w1)
        if step == min(3, half_n):
            acc1[...] = jnp.zeros(acc1.shape, F32)
            acc2[...] = jnp.zeros(acc2.shape, F32)

    RM = L + 12
    mix[...] = jnp.zeros(mix.shape, F32)
    top = lax.rem(L * gx - 6 + 2 * NX, NX)

    def correlate(rows_at, count, tiles):
        base = lax.rem(rows_at - top + 2 * NX, NX)

        def tile(t, carry):
            col = pl.multiple_of(tiles[0] + t * tiles[1], 16)
            parts = [
                [mix[m, pl.ds(pl.multiple_of(col + 8 * e, 8), 8), :] for e in range(2)] for m in range(RM)
            ]
            factors = {d: kd[base + (NX + d)] for d in range(1 - RM, count)}
            for r in range(count):
                value = lat[rows_at + r, pl.ds(col, 16), :].astype(F32)
                for m in range(RM):
                    for e in range(2):
                        parts[m][e] = parts[m][e] + value[8 * e : 8 * e + 8] * factors[r - m]
            for m in range(RM):
                for e in range(2):
                    mix[m, pl.ds(pl.multiple_of(col + 8 * e, 8), 8), :] = parts[m][e]
            return carry

        lax.fori_loop(0, tiles[2], tile, 0)

    center = (EDGE, 16, WC // 16)
    sides = (0, EDGE + WC, 2)
    correlate(L * gx, L, center)

    def cot_copy(i):
        rows_src = (slice(L - 3, L), slice(0, L), slice(0, 3))
        rows_dst = (slice(0, 3), slice(3, 3 + L), slice(3 + L, 6 + L))
        cols_src = (slice(WC - EDGE, WC), slice(0, WC), slice(0, EDGE))
        cols_dst = (slice(0, EDGE), slice(EDGE, EDGE + WC), slice(EDGE + WC, W))
        a, b = i // 3, i % 3
        target = ((down, gx, up)[a], (east, gy, west)[b])
        return copy(
            cot_in.at[rows_src[a], cols_src[b], :], cot.at[rows_dst[a], cols_dst[b], :],
            cot_s.at[i], cot_r.at[i], target,
        )

    def add_edges(block):
        for way in range(2):
            edge(way, block).wait_recv()
        correlate(L * block, L, sides)

    waiting = [gx]
    cots = [i for i in range(9) if i != 4]
    for step in range(1, half_n + 1):
        for h in range(2):
            for way in range(2):
                if goes(way, step, h):
                    ring(way, step, h).wait_recv()
                    if goes(way, step + 1, h):
                        ring(way, step + 1, h).start()
        if step < half_n:
            blocks = [at_pos(pos - step), at_pos(pos + step)]
        else:
            blocks = [at_pos(pos + step)]
        for block in blocks:
            for way in range(2):
                edge(way, block).start()
        if step == half_n:
            for i in cots:
                cot_copy(i).start()
        for block in blocks:
            correlate(L * block, L, center)
        for block in waiting:
            add_edges(block)
        waiting = blocks
        prepare(step)
    for block in waiting:
        add_edges(block)

    def flat(ref):
        return ref[...].reshape(-1, C)

    def widen(target, value, rows, dil):
        m = rows * W
        xf[8 : 8 + m, :] = value
        for q in range(3):
            at = 8 + (q - 1) * dil
            target[0:m, q * C : (q + 1) * C] = xf[at : at + m, :].astype(BF)

    def rows_dot(source, starts, weight, rows):
        taps = jnp.concatenate([source[at * W : (at + rows) * W, :] for at in starts], axis=1)
        return jnp.dot(taps, weight[...], preferred_element_type=F32)

    def weight_grad(source, starts, slope_own, p):
        at = starts[p]
        taps = jnp.concatenate(
            [source[(at + i) * W + EDGE : (at + i) * W + EDGE + WC, :] for i in range(L)], axis=0
        )
        return lax.dot_general(taps, slope_own, (((0,), (0,)), ((), ())), preferred_element_type=F32)

    def own(value, start):
        return jnp.concatenate(
            [value[(start + i) * W + EDGE : (start + i) * W + EDGE + WC, :] for i in range(L)], axis=0
        )

    for m in range(RM):
        row = lat[lax.rem(top + m, NX), :, :].astype(F32)
        mix[m] = (row + mix[m]).astype(BF).astype(F32)

    R1 = L + 10
    widen(xs, flat(mix), RM, D1)
    pre1[...] = rows_dot(xs, (0, 1, 2), w1, R1) + b1[...]
    v = pre1[...]
    mixed_in = mix[1 : 1 + R1].reshape(-1, C)
    hid[...] = (mixed_in + v * sigmoid(v)).astype(BF).astype(F32)
    R2 = L + 6
    widen(xh, hid[...], R1, D2)
    pre2 = rows_dot(xh, (0, 2, 4), w2, R2) + b2[...]
    own2 = own(pre2, 3)
    own_hid = own(hid, 5)
    pred[...] = (own_hid + own2 * sigmoid(own2)).astype(BF).reshape(L, WC, C)
    for i in cots:
        cot_copy(i).wait_recv()
    slope2 = (flat(cot).astype(F32) * slope_of(pre2)).astype(BF).astype(F32)
    own_slope2 = own(slope2, 3)
    grad2 = [weight_grad(xh, (3, 5, 7), own_slope2.astype(BF), p) for p in range(3)]
    SIZE = 9 * C
    first = min(acc1.shape[0], SIZE)

    def put_second(p):
        lo, hi = p * 3 * C, (p + 1) * 3 * C
        cut = min(max(first, lo), hi)
        if cut > lo:
            acc1[lo:cut, :] = grad2[p][: cut - lo]
        if cut < hi:
            acc2[cut - first : hi - first, :] = grad2[p][cut - lo :]

    for p in range(3):
        put_second(p)

    class Stream:
        pass

    streams = []
    for k in range(2):
        s = Stream()
        s.k = k
        s.ch = (CH1, CH2)[k]
        s.acc, s.hacc, s.qacc = (acc1, acc2)[k], (hacc1, hacc2)[k], (qacc1, qacc2)[k]
        s.sa, s.ra = (sa1, sa2)[k], (ra1, ra2)[k]
        s.sb, s.rb = (sb1, sb2)[k], (rb1, rb2)[k]
        s.sc, s.rc, s.og = (sc1, sc2)[k], (rc1, rc2)[k], (og1, og2)[k]
        s.quarter = GX * s.ch
        s.half = GA * s.quarter
        streams.append(s)

    def ds(at, size):
        return pl.ds(pl.multiple_of(at, 16), size)

    def p1(s):
        return copy(s.sa, s.ra, p1_s.at[s.k], p1_r.at[s.k], (gx, mate))

    def p2(s, d):
        other = lax.rem(ga + d, GA)
        return copy(s.sb.at[ds(other * s.quarter, s.quarter), :], s.rb.at[d],
                    p2_s.at[s.k, d], p2_r.at[s.k, d], (gx, 2 * other + core))

    def p3(s, d):
        other = lax.rem(gx + d, GX)
        return copy(s.sc.at[ds(other * s.ch, s.ch), :], s.rc.at[d],
                    p3_s.at[s.k, d], p3_r.at[s.k, d], (other, gy))

    def g3(s, d, send):
        owner = gx if send else lax.rem(gx + GX - d, GX)
        piece = s.og.at[ds(core * s.half + ga * s.quarter + owner * s.ch, s.ch), :]
        return copy(piece, piece, g3_s.at[s.k, d], g3_r.at[s.k, d], (lax.rem(gx + d, GX), gy))

    def g2(s, d, send):
        owner = ga if send else lax.rem(ga + GA - d, GA)
        piece = s.og.at[ds(core * s.half + owner * s.quarter, s.quarter), :]
        return copy(piece, piece, g2_s.at[s.k, d], g2_r.at[s.k, d],
                    (gx, 2 * lax.rem(ga + d, GA) + core))

    def g1(s, send):
        owner = core if send else 1 - core
        piece = s.og.at[ds(owner * s.half, s.half), :]
        return copy(piece, piece, g1_s.at[s.k], g1_r.at[s.k], (gx, mate))

    def begin(s):
        s.sa[...] = s.acc[ds((1 - core) * s.half, s.half), :].astype(BF)
        p1(s).start()

    def after_one(s):
        p1(s).wait_recv()
        total = s.acc[ds(core * s.half, s.half), :] + s.ra[...].astype(F32)
        s.hacc[...] = total
        s.sb[...] = total.astype(BF)
        for d in range(1, GA):
            p2(s, d).start()

    def after_two(s):
        total = s.hacc[ds(ga * s.quarter, s.quarter), :]
        for d in range(1, GA):
            p2(s, d).wait_recv()
            total = total + s.rb[d].astype(F32)
        s.qacc[...] = total
        s.sc[...] = total.astype(BF)
        for d in range(1, GX):
            p3(s, d).start()

    def after_three(s):
        total = s.qacc[ds(gx * s.ch, s.ch), :]
        for d in range(1, GX):
            p3(s, d).wait_recv()
            total = total + s.rc[d].astype(F32)
        s.og[ds(core * s.half + ga * s.quarter + gx * s.ch, s.ch), :] = total.astype(BF)
        for d in range(1, GX):
            g3(s, d, True).start()

    def gather_two(s):
        for d in range(1, GX):
            g3(s, d, False).wait_recv()
        for d in range(1, GA):
            g2(s, d, True).start()

    def gather_one(s):
        for d in range(1, GA):
            g2(s, d, False).wait_recv()
        g1(s, True).start()

    one, two = streams
    begin(one)

    R3 = L + 2
    widen(xg, slope2, R2, -D2)
    back2 = rows_dot(xg, (0, 2, 4), wt2, R3)
    grad_hid = flat(cot)[2 * W : (2 + R3) * W].astype(F32) + back2
    slope1 = (grad_hid * slope_of(pre1[4 * W : (4 + R3) * W, :])).astype(BF).astype(F32)
    after_one(one)
    own_slope1 = own(slope1, 1)
    shift = SIZE - first
    for p in range(3):
        lo = shift + p * 3 * C
        acc2[lo : lo + 3 * C, :] = weight_grad(xs, (5, 6, 7), own_slope1.astype(BF), p)
    widen(xg, slope1, R3, -D1)
    grad_mixed = grad_hid[W : (1 + L) * W] + rows_dot(xg, (0, 1, 2), wt1, L)
    mix[0:L, EDGE : EDGE + WC, :] = own(grad_mixed, 0).astype(BF).astype(F32).reshape(L, WC, C)
    misc = shift + SIZE

    def kernel_rows(part, carry):
        base = L * gx + 4 * part
        totals = [jnp.zeros((8, C), F32) for _ in range(4)]
        rows = [lax.rem(base + i, NX) for i in range(L + 3)]
        for t in range(WC // 16):
            cols = slice(EDGE + t * 16, EDGE + (t + 1) * 16)
            fields = [lat[row, cols, :].astype(F32) for row in rows]
            for i in range(L):
                for e in range(2):
                    at = EDGE + t * 16 + 8 * e
                    grad = mix[i, at : at + 8, :]
                    for o in range(4):
                        totals[o] = totals[o] + grad * fields[i + o][8 * e : 8 * e + 8]
        for o in range(4):
            acc2[pl.ds(misc + 4 * part + o, 1), :] = jnp.sum(totals[o], axis=0, keepdims=True)
        return carry

    lax.fori_loop(0, NX // 4, kernel_rows, 0)
    acc2[misc + NX : misc + NX + 1, :] = jnp.sum(own_slope1, axis=0, keepdims=True)
    acc2[misc + NX + 8 : misc + NX + 9, :] = jnp.sum(own_slope2, axis=0, keepdims=True)

    begin(two)
    after_two(one)
    after_one(two)
    after_three(one)
    after_two(two)
    gather_two(one)
    after_three(two)
    gather_one(one)
    gather_two(two)
    gather_one(two)
    g1(one, False).wait_recv()
    o2[0:first, :] = og1[0:first, :]
    g1(two, False).wait_recv()
    if first < SIZE:
        o2[first:SIZE, :] = og2[0:shift, :]
    o1[...] = og2[shift : shift + SIZE, :]
    orest[...] = og2[misc : misc + NX + 16, :]

    for step in range(1, half_n + 1):
        for h in range(2):
            for way in range(2):
                if goes(way, step, h):
                    ring(way, step, h).wait_send()

    def sent(block, carry):
        for way in range(2):
            edge(way, block).wait_send()
        return carry

    lax.fori_loop(0, GX, sent, 0)
    for i in cots:
        cot_copy(i).wait_send()
    for s in streams:
        p1(s).wait_send()
        for d in range(1, GA):
            p2(s, d).wait_send()
            g2(s, d, True).wait_send()
        for d in range(1, GX):
            p3(s, d).wait_send()
            g3(s, d, True).wait_send()
        g1(s, True).wait_send()


def closing(NX, pred, o2, o1, rest, pred_out, g1, gb1, g2, gb2, gk):
    pred_out[...] = pred[...]
    g1[...] = o1[...].astype(F32)
    g2[...] = o2[...].astype(F32)
    gk[...] = rest[0:NX, :].astype(F32)
    tail = rest[NX : NX + 16, :].astype(F32)
    gb1[...] = tail[0:1]
    gb2[...] = tail[8:9]


def per_device(latent, corr_kernel, w1, b1, w2, b2, cotangent):
    GX, GY = lax.axis_size("gx"), lax.axis_size("gy")
    L, WC, C = latent.shape
    NX = L * GX
    W = WC + 2 * EDGE
    N = GX * GY
    GA = GY // 2
    SIZE = 9 * C
    CH1 = max(16, SIZE // (16 * N) * 16)
    rest = SIZE - min(SIZE, CH1 * N) + SIZE + NX + 16
    CH2 = -(-rest // (16 * N)) * 16
    dma = pltpu.SemaphoreType.DMA

    def pair(shape_of, kind):
        return [pltpu.VMEM(shape_of(ch), kind) for ch in (CH1, CH2)]

    scratch = [
        pltpu.VMEM((NX, W, C), BF),
        pltpu.VMEM((L + 6, W, C), BF),
        pltpu.VMEM((3 * NX, 8, C), F32),
        pltpu.VMEM((L + 12, W, C), F32),
        pltpu.VMEM(((L + 12) * W + 16, C), F32),
        pltpu.VMEM(((L + 12) * W, 3 * C), BF),
        pltpu.VMEM(((L + 10) * W, 3 * C), BF),
        pltpu.VMEM(((L + 6) * W, 3 * C), BF),
        pltpu.VMEM(((L + 10) * W, C), F32),
        pltpu.VMEM(((L + 10) * W, C), F32),
        pltpu.VMEM((9 * C, C), BF),
        pltpu.VMEM((9 * C, C), BF),
        *pair(lambda ch: (N * ch, C), F32),
        *pair(lambda ch: (GA * GX * ch, C), F32),
        *pair(lambda ch: (GX * ch, C), F32),
        *pair(lambda ch: (GA * GX * ch, C), BF),
        *pair(lambda ch: (GA * GX * ch, C), BF),
        *pair(lambda ch: (GA * GX * ch, C), BF),
        *pair(lambda ch: (GA, GX * ch, C), BF),
        *pair(lambda ch: (GX * ch, C), BF),
        *pair(lambda ch: (GX, ch, C), BF),
        *pair(lambda ch: (N * ch, C), BF),
        dma((2, GX // 2, 2)), dma((2, GX // 2, 2)),
        dma((2, GX)), dma((2, GX)),
        dma((9,)), dma((9,)),
        dma((2,)), dma((2,)),
        dma((2, GA)), dma((2, GA)),
        dma((2, GX)), dma((2, GX)),
        dma((2, GX)), dma((2, GX)),
        dma((2, GA)), dma((2, GA)),
        dma((2,)), dma((2,)),
    ]
    vmem = pl.BlockSpec(memory_space=pltpu.VMEM)
    held = pl.pallas_call(
        functools.partial(kernel, GX, GY, L, WC, C, CH1, CH2),
        out_shape=(
            jax.ShapeDtypeStruct((L, WC, C), BF),
            jax.ShapeDtypeStruct((SIZE, C), BF),
            jax.ShapeDtypeStruct((SIZE, C), BF),
            jax.ShapeDtypeStruct((NX + 16, C), BF),
        ),
        in_specs=[vmem] * 7,
        out_specs=[vmem] * 4,
        scratch_shapes=scratch,
        compiler_params=pltpu.CompilerParams(
            collective_id=0, has_side_effects=True, vmem_limit_bytes=56 * 1024 * 1024
        ),
        cost_estimate=pl.CostEstimate(
            flops=2 * 6 * 10 * W * SIZE * C, bytes_accessed=4 * SIZE * C * 2, transcendentals=24 * W * C
        ),
    )(
        latent, corr_kernel, w1.reshape(9 * C, C), b1.reshape(1, C),
        w2.reshape(9 * C, C), b2.reshape(1, C), cotangent,
    )
    pred, g1, gb1, g2, gb2, gk = pl.pallas_call(
        functools.partial(closing, NX),
        out_shape=(
            jax.ShapeDtypeStruct((L, WC, C), BF),
            jax.ShapeDtypeStruct((SIZE, C), F32),
            jax.ShapeDtypeStruct((1, C), F32),
            jax.ShapeDtypeStruct((SIZE, C), F32),
            jax.ShapeDtypeStruct((1, C), F32),
            jax.ShapeDtypeStruct((NX, C), F32),
        ),
        in_specs=[vmem] * 4,
        out_specs=[vmem] * 6,
        compiler_params=pltpu.CompilerParams(vmem_limit_bytes=16 * 1024 * 1024),
    )(*held)
    shape = (3, 3, C, C)
    return (pred, g1.reshape(shape), gb1.reshape(C), g2.reshape(shape), gb2.reshape(C), gk)


def solution(mesh):
    in_specs = (P("gx", "gy", None), P(), P(), P(), P(), P(), P("gx", "gy", None))
    out_specs = (P("gx", "gy", None), P(), P(), P(), P(), P())
    return jax.shard_map(
        per_device, mesh=mesh, in_specs=in_specs, out_specs=out_specs, check_vma=False
    )
```
